32 devices in a mesh: dp: 16 (over z, x, core), tensor: 2 (over y).
Axes of the slice: x: 2, y: 2, z: 4, core: 2. Of those that a mesh axis runs over, the one named last changes fastest.
Arguments:
- layer_in: bfloat16 [4096, 1024], P(('dp', 'tensor')), may hold values from -6 to 6
- seq_lengths: int32 [16, 4], P('dp'), may hold values from 1 to 206, as said below
- attn_gain: float32 [1024], replicated, may hold values from 0.1 to 1.9
- query_gain: float32 [128], replicated, may hold values from 0.1 to 1.9
- key_gain: float32 [128], replicated, may hold values from 0.1 to 1.9
- query_weight: bfloat16 [1024, 2048], P('dp', 'tensor'), may hold values from -0.1875 to 0.1875
- key_matrix: bfloat16 [1024, 1024], P('dp', 'tensor'), may hold values from -0.1875 to 0.1875
- value_matrix: bfloat16 [1024, 1024], P('dp', 'tensor'), may hold values from -0.1875 to 0.1875
- output_weight: bfloat16 [2048, 1024], P('tensor', 'dp'), may hold values from -0.75 to 0.75
- mlp_gain: float32 [1024], replicated, may hold values from 0.1 to 1.9
- gate_weight: bfloat16 [1024, 3072], P('dp', 'tensor'), may hold values from -0.1875 to 0.1875
- up_weight: bfloat16 [1024, 3072], P('dp', 'tensor'), may hold values from -0.1875 to 0.1875
- down_weight: bfloat16 [3072, 1024], P('tensor', 'dp'), may hold values from -0.109375 to 0.109375
- out_grad: bfloat16 [4096, 1024], P(('dp', 'tensor')), may hold values from -6 to 6
Outputs:
- layer_out: bfloat16 [4096, 1024], P(('dp', 'tensor'))
- input_grad: bfloat16 [4096, 1024], P(('dp', 'tensor'))
- attn_gain_grad: float32 [1024], replicated
- query_gain_grad: float32 [128], replicated
- key_gain_grad: float32 [128], replicated
- query_weight_grad: float32 [1024, 2048], P('dp', 'tensor')
- key_weight_grad: float32 [1024, 1024], P('dp', 'tensor')
- value_weight_grad: float32 [1024, 1024], P('dp', 'tensor')
- output_weight_grad: float32 [2048, 1024], P('tensor', 'dp')
- mlp_gain_grad: float32 [1024], replicated
- gate_weight_grad: float32 [1024, 3072], P('dp', 'tensor')
- up_weight_grad: float32 [1024, 3072], P('dp', 'tensor')
- down_weight_grad: float32 [3072, 1024], P('tensor', 'dp')
The draws below stay inside these ranges and needn't reach their ends.
Inputs may be any that keep to these rules, and one draw needn't show every extreme that they name: `seq_lengths`: in each group the 4 lengths are positive and sum to at most 256, and to exactly 256 in some group; slots after the last sequence of a group are padding; the most is reached in some group.
All inputs are finite; a program needn't handle non-finite values.
Results may differ from the reference program's by a relative error of at most 0.018.
Values may be sent and summed in bfloat16 or wider, within the bound.
A program may use at most 128 MiB of HBM per device.

```python
import math
import jax
import jax.numpy as jnp
from jax import lax

MODEL_WIDTH = 1024
QUERY_HEADS = 16
KEY_VALUE_HEADS = 8
HEAD_SIZE = 128
FF = 3072
GROUP_SLOTS = 256
SEQS = 4
GROUPS = 16
TOKENS = 4096


def draw_seq_lengths(key, part):
    keys = jax.random.split(jax.random.fold_in(key, 17), 5)
    raw = jax.random.randint(keys[0], (GROUPS,), 0, GROUP_SLOTS // 8)
    fill = GROUP_SLOTS - (raw - jnp.min(raw))
    cut_one = jax.random.randint(keys[1], (GROUPS,), 1, GROUP_SLOTS // 4)
    cut_two = jax.random.randint(keys[2], (GROUPS,), 3 * GROUP_SLOTS // 4, 3 * GROUP_SLOTS // 4 + GROUP_SLOTS // 16)
    chosen = jax.random.randint(keys[4], (), 0, GROUPS)
    marked = jnp.arange(GROUPS) == chosen
    cut_one = jnp.where(marked, 1, cut_one)
    cut_two = jnp.where(marked, 3 * GROUP_SLOTS // 4 + GROUP_SLOTS // 16 - 1, cut_two)
    cut_three = jax.random.randint(keys[3], (GROUPS,), cut_two + 1, fill)
    lengths = jnp.stack([cut_one, cut_two - cut_one, cut_three - cut_two, fill - cut_three], 1)
    return lengths.astype(jnp.int32)


def strengthened(entries, rng, source, target, blocks, factor):
    def block_of(position):
        return (jnp.arange(entries.shape[position]) // (entries.shape[position] // blocks)).reshape((-1,) + (1,) * (entries.ndim - 1 - position))

    first = jax.random.permutation(rng, blocks)[block_of(target)]
    other_side = (block_of(target) + blocks // 2) % blocks
    return jnp.where((block_of(source) == first) | (block_of(source) == other_side), factor * entries, entries)


def shard_levels(rng, extent, cuts, low, high):
    factor_of = 1.0
    for axis_at, parts in cuts:
        draws = jax.random.uniform(jax.random.fold_in(jax.random.fold_in(rng, 6), axis_at), (parts,), jnp.float32, low / len(cuts), high / len(cuts))
        factor_of = factor_of * jnp.repeat(jnp.exp(draws), extent[axis_at] // parts).reshape((-1,) + (1,) * (len(extent) - 1 - axis_at))
    return factor_of


def centred(own_key, shape, deviation, reach, cuts=(), held_as=jnp.bfloat16):
    array = jax.random.normal(own_key, shape, jnp.float32) * deviation
    if len(cuts) > 0:
        array = shard_levels(own_key, shape, cuts, -0.22, 0.18) * array
    return jnp.clip(array, min=-reach, max=reach).astype(held_as)


def gaussian_with(own_key, extent, deviation, limit, pieces, heavy, held_as=jnp.bfloat16):
    array = deviation * jax.random.normal(own_key, extent, jnp.float32)
    if pieces:
        array = array * shard_levels(own_key, extent, pieces, -0.22, 0.18)
    return jnp.clip(strengthened(array, jax.random.fold_in(own_key, 3), *heavy), -limit, limit).astype(held_as)


def setup_inputs(seed: int = 0) -> dict:
    arg_keys = jax.random.split(jax.random.key(seed), 15)
    return {
        "layer_in": centred(arg_keys[0], (TOKENS, MODEL_WIDTH), 1.0, 6.0, ((0, 32),)),
        "seq_lengths": draw_seq_lengths(jax.random.fold_in(arg_keys[14], 71), 0),
        "attn_gain": jnp.clip(1.0 + 0.18 * jax.random.normal(arg_keys[2], (MODEL_WIDTH,), jnp.float32), 0.1, 1.9),
        "query_gain": jnp.clip(1.0 + 0.18 * jax.random.normal(arg_keys[3], (HEAD_SIZE,), jnp.float32), 0.1, 1.9),
        "key_gain": jnp.clip(1.0 + 0.18 * jax.random.normal(arg_keys[4], (HEAD_SIZE,), jnp.float32), 0.1, 1.9),
        "query_weight": centred(arg_keys[5], (MODEL_WIDTH, QUERY_HEADS * HEAD_SIZE), MODEL_WIDTH ** -0.5, 0.1875, ((0, 16), (1, 2))),
        "key_matrix": centred(arg_keys[6], (MODEL_WIDTH, KEY_VALUE_HEADS * HEAD_SIZE), MODEL_WIDTH ** -0.5, 0.1875, ((0, 16), (1, 2))),
        "value_matrix": centred(arg_keys[7], (MODEL_WIDTH, KEY_VALUE_HEADS * HEAD_SIZE), MODEL_WIDTH ** -0.5, 0.1875, ((0, 16), (1, 2))),
        "output_weight": centred(arg_keys[8], (QUERY_HEADS * HEAD_SIZE, MODEL_WIDTH), (QUERY_HEADS * HEAD_SIZE // 32) ** -0.5, 0.75, ((0, 2), (1, 16))),
        "mlp_gain": jnp.clip(1.0 + 0.18 * jax.random.normal(arg_keys[9], (MODEL_WIDTH,), jnp.float32), 0.1, 1.9),
        "gate_weight": centred(arg_keys[10], (MODEL_WIDTH, FF), MODEL_WIDTH ** -0.5, 0.1875, ((0, 16), (1, 2))),
        "up_weight": centred(arg_keys[11], (MODEL_WIDTH, FF), MODEL_WIDTH ** -0.5, 0.1875, ((0, 16), (1, 2))),
        "down_weight": centred(arg_keys[12], (FF, MODEL_WIDTH), FF ** -0.5, 0.109375, ((0, 2), (1, 16))),
        "out_grad": gaussian_with(arg_keys[13], (TOKENS, MODEL_WIDTH), 1.0, 6.0, ((0, 32),), (0, 1, 32, 2.75)),
    }


@jax.custom_vjp
def lower_precision(v):
    return lax.optimization_barrier(v.astype(jnp.bfloat16)).astype(jnp.float32)

@jax.custom_vjp
def lower_precision_back(v):
    return v

def low_keep(v):
    return (lower_precision(v), None)

def low_pass(kept, grad):
    return (grad,)

def back_keep(v):
    return (v, None)

def back_low(kept, grad):
    return (lower_precision(grad),)
lower_precision.defvjp(low_keep, low_pass)
lower_precision_back.defvjp(back_keep, back_low)
EPS = 1e-06
NEG = -1e+30
ROPE_BASE = 1000000.0

def matrix_product(a, b):
    return jnp.dot(a, b, precision=lax.Precision.HIGHEST, preferred_element_type=jnp.float32)

def normalize(v, gain):
    return v * lax.rsqrt(lax.optimization_barrier(jnp.mean(v * v, -1, keepdims=True)) + EPS) * gain

def layout(lengths_row):
    slots = jnp.arange(GROUP_SLOTS, dtype=jnp.int32)
    ends = jnp.cumsum(lengths_row).astype(jnp.int32)
    seg = lax.optimization_barrier(jnp.sum((slots[:, None] >= ends[None, :]).astype(jnp.int32), 1))
    starts = jnp.concatenate([jnp.zeros((1,), jnp.int32), ends])
    which = seg[:, None] == jnp.arange(SEQS + 1, dtype=jnp.int32)[None, :]
    start_of = lax.optimization_barrier(jnp.sum(jnp.where(which, starts[None, :], 0), 1)).astype(jnp.int32)
    return (slots, seg, slots - start_of)

def rotate(v, cosine, sine):
    half = HEAD_SIZE // 2
    first = v[..., :half]
    second = v[..., half:]
    cos_b = cosine[:, None, :]
    sin_b = sine[:, None, :]
    return jnp.concatenate([first * cos_b - second * sin_b, second * cos_b + first * sin_b], -1)

def group_layer(params, x, lengths_row):
    attn_gain, query_gain, key_gain, wq, key_projection_weight, value_projection_weight, wo, mlp_gain, wg, wu, wd = params
    slots, seg, pos = layout(lengths_row)
    inv = ROPE_BASE ** (-2.0 * jnp.arange(HEAD_SIZE // 2, dtype=jnp.float32) / HEAD_SIZE)
    angle = pos.astype(jnp.float32)[:, None] * inv[None, :]
    cosine = jnp.cos(angle)
    sine = jnp.sin(angle)
    first_activation = lower_precision(normalize(x, attn_gain))
    q_raw = lower_precision_back(matrix_product(first_activation, wq)).reshape(GROUP_SLOTS, QUERY_HEADS, HEAD_SIZE)
    key_unrotated = lower_precision_back(matrix_product(first_activation, key_projection_weight)).reshape(GROUP_SLOTS, KEY_VALUE_HEADS, HEAD_SIZE)
    query_rotated = lower_precision(rotate(normalize(q_raw, query_gain), cosine, sine))
    k_rot = lower_precision(rotate(normalize(key_unrotated, key_gain), cosine, sine))
    value_rows = lower_precision(lower_precision_back(matrix_product(first_activation, value_projection_weight))).reshape(GROUP_SLOTS, KEY_VALUE_HEADS, HEAD_SIZE)
    query_grouped = query_rotated.reshape(GROUP_SLOTS, KEY_VALUE_HEADS, QUERY_HEADS // KEY_VALUE_HEADS, HEAD_SIZE)
    raw = jnp.einsum('qhgd,khd->hgqk', query_grouped, k_rot, precision=lax.Precision.HIGHEST) * HEAD_SIZE ** (-0.5)
    scores = lower_precision_back(raw)
    allowed = (seg[:, None] == seg[None, :]) & (slots[None, :] <= slots[:, None])
    masked = jnp.where(allowed, scores, NEG)
    top = lax.optimization_barrier(jnp.max(masked, -1, keepdims=True))
    expo = jnp.exp(masked - top)
    probs = expo / lax.optimization_barrier(jnp.sum(expo, -1, keepdims=True))
    attended = jnp.einsum('hgqk,khd->qhgd', lower_precision(probs), value_rows, precision=lax.Precision.HIGHEST)
    attended = lower_precision(lower_precision_back(attended)).reshape(GROUP_SLOTS, QUERY_HEADS * HEAD_SIZE)
    mid = x + lower_precision_back(matrix_product(attended, wo))
    a2 = lower_precision(normalize(mid, mlp_gain))
    gate = lower_precision_back(matrix_product(a2, wg))
    up = lower_precision_back(matrix_product(a2, wu))
    act = lower_precision(jax.nn.sigmoid(gate) * gate * up)
    return mid + lower_precision_back(matrix_product(act, wd))

def reference(layer_in, seq_lengths, attn_gain, query_gain, key_gain, query_weight, key_matrix, value_matrix, output_weight, mlp_gain, gate_weight, up_weight, down_weight, out_grad):
    per = math.gcd(GROUPS, max(1, 4096 // GROUP_SLOTS))
    lengths = seq_lengths.reshape(GROUPS // per, per, SEQS)

    def forward(x, *params):
        xs = x.reshape(GROUPS // per, per, GROUP_SLOTS, MODEL_WIDTH)

        def step(item):
            return jax.vmap(lambda xg, lg: group_layer(params, xg, lg))(item[0], item[1])
        ys = lax.map(jax.checkpoint(step), (xs, lengths))
        return ys.reshape(GROUPS * GROUP_SLOTS, MODEL_WIDTH)
    primals = (layer_in.astype(jnp.float32), attn_gain.astype(jnp.float32), query_gain.astype(jnp.float32), key_gain.astype(jnp.float32), query_weight.astype(jnp.float32), key_matrix.astype(jnp.float32), value_matrix.astype(jnp.float32), output_weight.astype(jnp.float32), mlp_gain.astype(jnp.float32), gate_weight.astype(jnp.float32), up_weight.astype(jnp.float32), down_weight.astype(jnp.float32))
    out, pull = jax.vjp(forward, *primals)
    grads = pull(out_grad.astype(jnp.float32))
    return (out.astype(jnp.bfloat16), grads[0].astype(jnp.bfloat16), grads[1], grads[2], grads[3], grads[4], grads[5], grads[6], grads[7], grads[8], grads[9], grads[10], grads[11])
```

```python
import jax
import jax.numpy as jnp
from jax import lax
from jax.sharding import PartitionSpec as P

HEAD_SIZE = 128


EPS = 1e-06
NEG = -1e30
ROPE_BASE = 1000000.0


def normalize(v, gain):
    return v * lax.rsqrt(jnp.mean(v * v, -1, keepdims=True) + EPS) * gain


def layout(lengths_row, slots):
    ends = jnp.cumsum(lengths_row)
    seg = jnp.sum((slots[:, None] >= ends[None, :]).astype(jnp.int32), 1)
    starts = jnp.concatenate([jnp.zeros((1,), jnp.int32), ends])
    which = seg[:, None] == jnp.arange(starts.shape[0], dtype=jnp.int32)[None, :]
    start_of = jnp.sum(jnp.where(which, starts[None, :], 0), 1)
    return (seg, slots - start_of)


def swap(v):
    return lax.ppermute(v, "tensor", [(0, 1), (1, 0)])


def pair_sum(part):
    other = swap(part).astype(jnp.float32)
    half = part.shape[0] // 2
    return part.astype(jnp.float32) + jnp.concatenate([other[half:], other[:half]], axis=0)


def rotate(v, cosine, sine):
    half = v.shape[-1] // 2
    first = v[..., :half]
    second = v[..., half:]
    cos_b = cosine[:, None, :]
    sin_b = sine[:, None, :]
    return jnp.concatenate([first * cos_b - second * sin_b, second * cos_b + first * sin_b], -1)


def head_prep(raw, gain, cosine, sine, heads):
    shaped = raw.reshape(raw.shape[0], heads, HEAD_SIZE)
    return rotate(normalize(shaped, gain), cosine, sine)


def matrix_product(a, b):
    return jnp.dot(a, b, preferred_element_type=jnp.float32)


def by_rows(a, b):
    return lax.dot_general(a, b, (((0,), (0,)), ((), ())), preferred_element_type=jnp.float32)


def by_cols(a, b):
    return lax.dot_general(a, b, (((1,), (1,)), ((), ())), preferred_element_type=jnp.float32)


def shards(
    layer_in,
    seq_lengths,
    attn_gain,
    query_gain,
    key_gain,
    query_weight,
    key_matrix,
    value_matrix,
    output_weight,
    mlp_gain,
    gate_weight,
    up_weight,
    down_weight,
    out_grad,
):
    bf = jnp.bfloat16
    f32 = jnp.float32
    q_heads = query_weight.shape[1] // HEAD_SIZE
    kv_heads = key_matrix.shape[1] // HEAD_SIZE
    group = q_heads // kv_heads
    scale = HEAD_SIZE ** (-0.5)
    own = layer_in.shape[0]
    count = 2 * own
    q_cols, k_cols, units = query_weight.shape[1], key_matrix.shape[1], gate_weight.shape[1]
    qkv_cols = q_cols + 2 * k_cols

    attn_pack = jnp.concatenate(
        [query_weight, key_matrix, value_matrix, output_weight.T], axis=1
    )
    mlp_pack = jnp.concatenate([gate_weight, up_weight, down_weight.T], axis=1)
    w_attn = lax.all_gather(attn_pack, "dp", axis=0, tiled=True)
    w_attn, mlp_pack = lax.optimization_barrier((w_attn, mlp_pack))
    w_mlp = lax.all_gather(mlp_pack, "dp", axis=0, tiled=True)
    w_qkv = w_attn[:, :qkv_cols]
    wo_t = w_attn[:, qkv_cols:]
    w_gu = w_mlp[:, : 2 * units]
    wd_t = w_mlp[:, 2 * units :]

    both = jnp.concatenate([layer_in, out_grad], axis=1)
    both = jnp.concatenate([both, swap(both)], axis=0)
    width = layer_in.shape[1]
    residual = both[:, :width].astype(f32)
    dy_full = both[:, width:]
    me = lax.axis_index("tensor")
    steps = jnp.arange(own, dtype=jnp.int32)
    slots = jnp.concatenate([me * own + steps, (1 - me) * own + steps])
    seg, pos = layout(seq_lengths[0], slots)
    inv = ROPE_BASE ** (-2.0 * jnp.arange(HEAD_SIZE // 2, dtype=f32) / HEAD_SIZE)
    angle = pos.astype(f32)[:, None] * inv[None, :]
    cosine = jnp.cos(angle)
    sine = jnp.sin(angle)
    allowed = (seg[:, None] == seg[None, :]) & (slots[None, :] <= slots[:, None])

    r_in = lax.rsqrt(jnp.mean(residual * residual, -1, keepdims=True) + EPS)
    a1_full = (residual * r_in * attn_gain).astype(bf)
    qkv = matrix_product(a1_full, w_qkv)
    q_raw = qkv[:, :q_cols]
    key_unrotated = qkv[:, q_cols : q_cols + k_cols]
    q_bf = (
        head_prep(q_raw, query_gain, cosine, sine, q_heads)
        .astype(bf)
        .reshape(count, kv_heads, group, HEAD_SIZE)
    )
    k_bf = head_prep(key_unrotated, key_gain, cosine, sine, kv_heads).astype(bf)
    v_bf = qkv[:, q_cols + k_cols :].astype(bf).reshape(count, kv_heads, HEAD_SIZE)

    raw = jnp.einsum("qhgd,khd->hgqk", q_bf, k_bf, preferred_element_type=f32) * scale
    masked = jnp.where(allowed, raw, NEG)
    top = jnp.max(masked, -1, keepdims=True)
    log_total = top + jnp.log(jnp.sum(jnp.exp(masked - top), -1, keepdims=True))
    probs = jnp.exp(masked - log_total)
    probs_bf = probs.astype(bf)
    attended = jnp.einsum("hgqk,khd->qhgd", probs_bf, v_bf, preferred_element_type=f32)
    attended_bf = attended.reshape(count, q_heads * HEAD_SIZE).astype(bf)
    attn_part = by_cols(attended_bf, wo_t).astype(bf)
    middle = residual + pair_sum(attn_part)

    r_mid = lax.rsqrt(jnp.mean(middle * middle, -1, keepdims=True) + EPS)
    a2_full = (middle * r_mid * mlp_gain).astype(bf)
    gate_up = matrix_product(a2_full, w_gu)
    gate = gate_up[:, :units]
    upward = gate_up[:, units:]
    sigma = jax.nn.sigmoid(gate)
    act = (gate * sigma * upward).astype(bf)
    d_act = matrix_product(dy_full, wd_t)
    d_gate = (d_act * upward * sigma * (1.0 + gate * (1.0 - sigma))).astype(bf)
    d_up = (d_act * gate * sigma).astype(bf)
    d_gate_up = jnp.concatenate([d_gate, d_up], axis=1)
    d_a2_part = by_cols(d_gate_up, w_gu).astype(bf)
    d_a2 = pair_sum(d_a2_part)
    mlp_grads = jnp.concatenate(
        [by_rows(a2_full, d_gate_up).astype(bf), by_rows(dy_full, act).astype(bf)], axis=1
    )
    mlp_grads = lax.psum_scatter(mlp_grads, "dp", scatter_dimension=0, tiled=True)

    mlp_part = by_cols(act, wd_t)
    mlp_sum = mlp_part[:own] + swap(mlp_part[own:].astype(bf)).astype(f32)
    layer_out = (middle[:own] + mlp_sum).astype(bf)

    scaled = d_a2 * mlp_gain
    d_middle = (
        dy_full.astype(f32)
        + r_mid * scaled
        - middle * (r_mid * r_mid * r_mid) * jnp.mean(scaled * middle, -1, keepdims=True)
    )
    mlp_gain_part = jnp.sum(d_a2[:own] * middle[:own] * r_mid[:own], 0)
    dh_full = d_middle.astype(bf)
    d_att = matrix_product(dh_full, wo_t).astype(bf).reshape(count, kv_heads, group, HEAD_SIZE)
    d_probs = jnp.einsum("qhgd,khd->hgqk", d_att, v_bf, preferred_element_type=f32)
    delta = jnp.sum(d_probs * probs, -1, keepdims=True)
    d_scores = (probs * (d_probs - delta)).astype(bf)
    d_q_rot = (
        jnp.einsum("hgqk,khd->qhgd", d_scores, k_bf, preferred_element_type=f32) * scale
    ).reshape(count, q_heads, HEAD_SIZE)
    d_k_rot = jnp.einsum("hgqk,qhgd->khd", d_scores, q_bf, preferred_element_type=f32) * scale
    d_v_raw = (
        jnp.einsum("hgqk,qhgd->khd", probs_bf, d_att, preferred_element_type=f32)
        .reshape(count, kv_heads * HEAD_SIZE)
        .astype(bf)
    )
    _, pull_query = jax.vjp(
        lambda raw, gain: head_prep(raw, gain, cosine, sine, q_heads), q_raw, query_gain
    )
    d_q_raw, query_gain_part = pull_query(d_q_rot)
    _, pull_key = jax.vjp(
        lambda raw, gain: head_prep(raw, gain, cosine, sine, kv_heads), key_unrotated, key_gain
    )
    d_k_raw, key_gain_part = pull_key(d_k_rot)
    d_qkv = jnp.concatenate([d_q_raw.astype(bf), d_k_raw.astype(bf), d_v_raw], axis=1)
    attn_grads = jnp.concatenate(
        [by_rows(a1_full, d_qkv).astype(bf), by_rows(dh_full, attended_bf).astype(bf)], axis=1
    )
    attn_grads = lax.psum_scatter(attn_grads, "dp", scatter_dimension=0, tiled=True)

    d_a1_part = by_cols(d_qkv, w_qkv)
    d_a1 = d_a1_part[:own] + swap(d_a1_part[own:].astype(bf)).astype(f32)
    x_own, r_own = residual[:own], r_in[:own]
    scaled = d_a1 * attn_gain
    input_grad = (
        d_middle[:own]
        + r_own * scaled
        - x_own * (r_own * r_own * r_own) * jnp.mean(scaled * x_own, -1, keepdims=True)
    ).astype(bf)
    attn_gain_part = jnp.sum(d_a1 * x_own * r_own, 0)
    gains = lax.psum(
        (attn_gain_part, query_gain_part, key_gain_part, mlp_gain_part), ("dp", "tensor")
    )
    attn_grads = attn_grads.astype(f32)
    mlp_grads = mlp_grads.astype(f32)
    return (
        layer_out,
        input_grad,
        gains[0],
        gains[1],
        gains[2],
        attn_grads[:, :q_cols],
        attn_grads[:, q_cols : q_cols + k_cols],
        attn_grads[:, q_cols + k_cols : qkv_cols],
        attn_grads[:, qkv_cols:].T,
        gains[3],
        mlp_grads[:, :units],
        mlp_grads[:, units : 2 * units],
        mlp_grads[:, 2 * units :].T,
    )


def solution(mesh):
    placed = (
        P(("dp", "tensor"), None),
        P("dp", None),
        P(),
        P(),
        P(),
        P("dp", "tensor"),
        P("dp", "tensor"),
        P("dp", "tensor"),
        P("tensor", "dp"),
        P(),
        P("dp", "tensor"),
        P("dp", "tensor"),
        P("tensor", "dp"),
        P(("dp", "tensor"), None),
    )
    return jax.shard_map(
        shards,
        mesh=mesh,
        in_specs=placed,
        out_specs=(
            P(("dp", "tensor"), None),
            P(("dp", "tensor"), None),
            P(),
            P(),
            P(),
            P("dp", "tensor"),
            P("dp", "tensor"),
            P("dp", "tensor"),
            P("tensor", "dp"),
            P(),
            P("dp", "tensor"),
            P("dp", "tensor"),
            P("tensor", "dp"),
        ),
        check_vma=False,
    )
```

```python
import jax
import jax.numpy as jnp
from jax import lax
from jax.sharding import PartitionSpec as P

HEAD_SIZE = 128


EPS = 1e-06
NEG = -1e30
ROPE_BASE = 1000000.0


def normalize(v, gain):
    return v * lax.rsqrt(jnp.mean(v * v, -1, keepdims=True) + EPS) * gain


def layout(lengths_row, slots):
    ends = jnp.cumsum(lengths_row)
    seg = jnp.sum((slots[:, None] >= ends[None, :]).astype(jnp.int32), 1)
    starts = jnp.concatenate([jnp.zeros((1,), jnp.int32), ends])
    which = seg[:, None] == jnp.arange(starts.shape[0], dtype=jnp.int32)[None, :]
    start_of = jnp.sum(jnp.where(which, starts[None, :], 0), 1)
    return (seg, slots - start_of)


def swap(v):
    return lax.ppermute(v, "tensor", [(0, 1), (1, 0)])


def pair_sum(part):
    other = swap(part).astype(jnp.float32)
    half = part.shape[0] // 2
    return part.astype(jnp.float32) + jnp.concatenate([other[half:], other[:half]], axis=0)


def rotate(v, cosine, sine):
    half = v.shape[-1] // 2
    first = v[..., :half]
    second = v[..., half:]
    cos_b = cosine[:, None, :]
    sin_b = sine[:, None, :]
    return jnp.concatenate([first * cos_b - second * sin_b, second * cos_b + first * sin_b], -1)


def head_prep(raw, gain, cosine, sine, heads):
    shaped = raw.reshape(raw.shape[0], heads, HEAD_SIZE)
    return rotate(normalize(shaped, gain), cosine, sine)


def matrix_product(a, b):
    return jnp.dot(a, b, preferred_element_type=jnp.float32)


def by_rows(a, b):
    return lax.dot_general(a, b, (((0,), (0,)), ((), ())), preferred_element_type=jnp.float32)


def by_cols(a, b):
    return lax.dot_general(a, b, (((1,), (1,)), ((), ())), preferred_element_type=jnp.float32)


def shards(
    layer_in,
    seq_lengths,
    attn_gain,
    query_gain,
    key_gain,
    query_weight,
    key_matrix,
    value_matrix,
    output_weight,
    mlp_gain,
    gate_weight,
    up_weight,
    down_weight,
    out_grad,
):
    bf = jnp.bfloat16
    f32 = jnp.float32
    q_heads = query_weight.shape[1] // HEAD_SIZE
    kv_heads = key_matrix.shape[1] // HEAD_SIZE
    group = q_heads // kv_heads
    scale = HEAD_SIZE ** (-0.5)
    own = layer_in.shape[0]
    count = 2 * own
    q_cols, k_cols, units = query_weight.shape[1], key_matrix.shape[1], gate_weight.shape[1]
    qkv_cols = q_cols + 2 * k_cols

    attn_pack = jnp.concatenate(
        [query_weight, key_matrix, value_matrix, output_weight.T], axis=1
    )
    mlp_pack = jnp.concatenate([gate_weight, up_weight, down_weight.T], axis=1)
    w_attn = lax.all_gather(attn_pack, "dp", axis=0, tiled=True)

    both = jnp.concatenate([layer_in, out_grad], axis=1)
    both = jnp.concatenate([both, swap(both)], axis=0)
    w_attn, mlp_pack, both = lax.optimization_barrier((w_attn, mlp_pack, both))
    w_mlp = lax.all_gather(mlp_pack, "dp", axis=0, tiled=True)
    w_qkv = w_attn[:, :qkv_cols]
    wo_t = w_attn[:, qkv_cols:]
    w_gu = w_mlp[:, : 2 * units]
    wd_t = w_mlp[:, 2 * units :]
    width = layer_in.shape[1]
    residual = both[:, :width].astype(f32)
    dy_full = both[:, width:]
    me = lax.axis_index("tensor")
    steps = jnp.arange(own, dtype=jnp.int32)
    slots = jnp.concatenate([me * own + steps, (1 - me) * own + steps])
    seg, pos = layout(seq_lengths[0], slots)
    inv = ROPE_BASE ** (-2.0 * jnp.arange(HEAD_SIZE // 2, dtype=f32) / HEAD_SIZE)
    angle = pos.astype(f32)[:, None] * inv[None, :]
    cosine = jnp.cos(angle)
    sine = jnp.sin(angle)
    allowed = (seg[:, None] == seg[None, :]) & (slots[None, :] <= slots[:, None])

    r_in = lax.rsqrt(jnp.mean(residual * residual, -1, keepdims=True) + EPS)
    a1_full = (residual * r_in * attn_gain).astype(bf)
    qkv = matrix_product(a1_full, w_qkv)
    q_raw = qkv[:, :q_cols]
    key_unrotated = qkv[:, q_cols : q_cols + k_cols]
    q_bf = (
        head_prep(q_raw, query_gain, cosine, sine, q_heads)
        .astype(bf)
        .reshape(count, kv_heads, group, HEAD_SIZE)
    )
    k_bf = head_prep(key_unrotated, key_gain, cosine, sine, kv_heads).astype(bf)
    v_bf = qkv[:, q_cols + k_cols :].astype(bf).reshape(count, kv_heads, HEAD_SIZE)

    raw = jnp.einsum("qhgd,khd->hgqk", q_bf, k_bf, preferred_element_type=f32) * scale
    masked = jnp.where(allowed, raw, NEG)
    top = jnp.max(masked, -1, keepdims=True)
    log_total = top + jnp.log(jnp.sum(jnp.exp(masked - top), -1, keepdims=True))
    probs = jnp.exp(masked - log_total)
    probs_bf = probs.astype(bf)
    attended = jnp.einsum("hgqk,khd->qhgd", probs_bf, v_bf, preferred_element_type=f32)
    attended_bf = attended.reshape(count, q_heads * HEAD_SIZE).astype(bf)
    attn_part = by_cols(attended_bf, wo_t).astype(bf)
    middle = residual + pair_sum(attn_part)

    r_mid = lax.rsqrt(jnp.mean(middle * middle, -1, keepdims=True) + EPS)
    a2_full = (middle * r_mid * mlp_gain).astype(bf)
    gate_up = matrix_product(a2_full, w_gu)
    gate = gate_up[:, :units]
    upward = gate_up[:, units:]
    sigma = jax.nn.sigmoid(gate)
    act = (gate * sigma * upward).astype(bf)
    d_act = matrix_product(dy_full, wd_t)
    d_gate = (d_act * upward * sigma * (1.0 + gate * (1.0 - sigma))).astype(bf)
    d_up = (d_act * gate * sigma).astype(bf)
    d_gate_up = jnp.concatenate([d_gate, d_up], axis=1)
    d_a2_part = by_cols(d_gate_up, w_gu).astype(bf)
    d_a2 = pair_sum(d_a2_part)
    mlp_grads = jnp.concatenate(
        [by_rows(a2_full, d_gate_up).astype(bf), by_rows(dy_full, act).astype(bf)], axis=1
    )
    d_a2, mlp_grads = lax.optimization_barrier((d_a2, mlp_grads))
    mlp_grads = lax.psum_scatter(mlp_grads, "dp", scatter_dimension=0, tiled=True)

    mlp_part = by_cols(act, wd_t)
    mlp_sum = mlp_part[:own] + swap(mlp_part[own:].astype(bf)).astype(f32)
    layer_out = (middle[:own] + mlp_sum).astype(bf)

    scaled = d_a2 * mlp_gain
    d_middle = (
        dy_full.astype(f32)
        + r_mid * scaled
        - middle * (r_mid * r_mid * r_mid) * jnp.mean(scaled * middle, -1, keepdims=True)
    )
    mlp_gain_part = jnp.sum(d_a2[:own] * middle[:own] * r_mid[:own], 0)
    dh_full = d_middle.astype(bf)
    d_att = matrix_product(dh_full, wo_t).astype(bf).reshape(count, kv_heads, group, HEAD_SIZE)
    d_probs = jnp.einsum("qhgd,khd->hgqk", d_att, v_bf, preferred_element_type=f32)
    delta = jnp.sum(d_probs * probs, -1, keepdims=True)
    d_scores = (probs * (d_probs - delta)).astype(bf)
    d_q_rot = (
        jnp.einsum("hgqk,khd->qhgd", d_scores, k_bf, preferred_element_type=f32) * scale
    ).reshape(count, q_heads, HEAD_SIZE)
    d_k_rot = jnp.einsum("hgqk,qhgd->khd", d_scores, q_bf, preferred_element_type=f32) * scale
    d_v_raw = (
        jnp.einsum("hgqk,qhgd->khd", probs_bf, d_att, preferred_element_type=f32)
        .reshape(count, kv_heads * HEAD_SIZE)
        .astype(bf)
    )
    _, pull_query = jax.vjp(
        lambda raw, gain: head_prep(raw, gain, cosine, sine, q_heads), q_raw, query_gain
    )
    d_q_raw, query_gain_part = pull_query(d_q_rot)
    _, pull_key = jax.vjp(
        lambda raw, gain: head_prep(raw, gain, cosine, sine, kv_heads), key_unrotated, key_gain
    )
    d_k_raw, key_gain_part = pull_key(d_k_rot)
    d_qkv = jnp.concatenate([d_q_raw.astype(bf), d_k_raw.astype(bf), d_v_raw], axis=1)
    attn_grads = jnp.concatenate(
        [by_rows(a1_full, d_qkv).astype(bf), by_rows(dh_full, attended_bf).astype(bf)], axis=1
    )
    attn_grads = lax.psum_scatter(attn_grads, "dp", scatter_dimension=0, tiled=True)

    d_a1_part = by_cols(d_qkv, w_qkv)
    d_a1 = d_a1_part[:own] + swap(d_a1_part[own:].astype(bf)).astype(f32)
    x_own, r_own = residual[:own], r_in[:own]
    scaled = d_a1 * attn_gain
    input_grad = (
        d_middle[:own]
        + r_own * scaled
        - x_own * (r_own * r_own * r_own) * jnp.mean(scaled * x_own, -1, keepdims=True)
    ).astype(bf)
    attn_gain_part = jnp.sum(d_a1 * x_own * r_own, 0)
    gains = lax.psum(
        (attn_gain_part, query_gain_part, key_gain_part, mlp_gain_part), ("dp", "tensor")
    )
    attn_grads = attn_grads.astype(f32)
    mlp_grads = mlp_grads.astype(f32)
    return (
        layer_out,
        input_grad,
        gains[0],
        gains[1],
        gains[2],
        attn_grads[:, :q_cols],
        attn_grads[:, q_cols : q_cols + k_cols],
        attn_grads[:, q_cols + k_cols : qkv_cols],
        attn_grads[:, qkv_cols:].T,
        gains[3],
        mlp_grads[:, :units],
        mlp_grads[:, units : 2 * units],
        mlp_grads[:, 2 * units :].T,
    )


def solution(mesh):
    placed = (
        P(("dp", "tensor"), None),
        P("dp", None),
        P(),
        P(),
        P(),
        P("dp", "tensor"),
        P("dp", "tensor"),
        P("dp", "tensor"),
        P("tensor", "dp"),
        P(),
        P("dp", "tensor"),
        P("dp", "tensor"),
        P("tensor", "dp"),
        P(("dp", "tensor"), None),
    )
    return jax.shard_map(
        shards,
        mesh=mesh,
        in_specs=placed,
        out_specs=(
            P(("dp", "tensor"), None),
            P(("dp", "tensor"), None),
            P(),
            P(),
            P(),
            P("dp", "tensor"),
            P("dp", "tensor"),
            P("dp", "tensor"),
            P("tensor", "dp"),
            P(),
            P("dp", "tensor"),
            P("dp", "tensor"),
            P("tensor", "dp"),
        ),
        check_vma=False,
    )
```
